256 devices in a mesh: dp: 64 (over z, y_hi, x), mp: 4 (over y_lo, core).
Axes of the slice: x: 4, y: 4 (y_hi: 2, y_lo: 2; y = y_hi * 2 + y_lo), z: 8, core: 2. Of those that a mesh axis runs over, the one named last changes fastest.
Arguments:
- hidden: bfloat16 [65536, 4608], P('dp', 'mp'), may hold values from -6 to 6
- out_grad: bfloat16 [65536, 2304], P(('dp', 'mp')), may hold values from -0.1875 to 0.1875
- momentum: bfloat16 [147456, 4608], P('dp', 'mp'), may hold values from -6 to 6
Outputs:
- fresh_momentum: bfloat16 [147456, 4608], P('dp', 'mp')
- update: bfloat16 [2304, 4608], P('dp', 'mp')
The draws below stay inside these ranges and needn't reach their ends.
All inputs are finite; a program needn't handle non-finite values.
Results may differ from the reference program's by a relative error of at most 0.003.
Values may be sent and summed in bfloat16 or wider, within the bound.
A program may use at most 192 MiB of HBM per device.

```python
import jax
import jax.numpy as jnp
from jax import lax

D_WIN = 2304
TOK_REP = 1024
GROUP = 64
BAND = 16
HIDDEN_SIZE = 4608
N_DP = 64


def levels(rng, shape, pieces, low, top_value):
    level = 1.0
    for dim, shards_of in pieces:
        heights = jax.random.uniform(jax.random.fold_in(jax.random.fold_in(rng, 6), dim), (shards_of,), jnp.float32, low / len(pieces), top_value / len(pieces))
        level = level * jnp.repeat(jnp.exp(heights), shape[dim] // shards_of).reshape((-1,) + (1,) * (len(shape) - 1 - dim))
    return level


def centred(key, extent, width, limit, split=(), kind=jnp.bfloat16):
    array = width * jax.random.normal(key, extent, jnp.float32)
    if split:
        array = array * levels(key, extent, split, -0.22, 0.18)
    return jnp.clip(array, -limit, limit).astype(kind)


def setup_inputs(seed: int = 0) -> dict:
    key_list = jax.random.split(jax.random.key(seed), 4)
    return {
        "hidden": centred(key_list[0], (N_DP * TOK_REP, HIDDEN_SIZE), 1.0, 6.0, ((0, 64), (1, 4))),
        "out_grad": centred(key_list[1], (N_DP * TOK_REP, D_WIN), TOK_REP ** -0.5, 0.1875, ((0, 256),)),
        "momentum": centred(key_list[2], (N_DP * D_WIN, HIDDEN_SIZE), 1.0, 6.0, ((0, 64), (1, 4))),
    }


DECAY = 0.9
highest = lax.Precision.HIGHEST

def dct_entry(frequency, position):
    norm_scale = jnp.where(frequency == 0, jnp.sqrt(1.0 / GROUP), jnp.sqrt(2.0 / GROUP))
    return norm_scale * jnp.cos(jnp.pi * (2.0 * position + 1.0) * frequency / (2.0 * GROUP))

def band_table():
    frequency = jnp.arange(BAND, dtype=jnp.float32)[:, None]
    position = jnp.arange(GROUP, dtype=jnp.float32)[None, :]
    return dct_entry(frequency, position)

def forward_band(moment, band_tab):
    row_total, col_total = moment.shape
    blocks = moment.reshape(row_total // GROUP, GROUP, col_total // GROUP, GROUP)
    lefted = jnp.einsum('ai,ricj->racj', band_tab, blocks, precision=highest)
    return jnp.einsum('racj,bj->racb', lefted, band_tab, precision=highest)

def inverse_band(band_coef, band_tab):
    righted = jnp.einsum('racb,bj->racj', band_coef, band_tab, precision=highest)
    restored = jnp.einsum('ai,racj->ricj', band_tab, righted, precision=highest)
    return restored.reshape(band_coef.shape[0] * GROUP, band_coef.shape[2] * GROUP)

def reference(hidden, out_grad, momentum):
    band_tab = band_table()
    hid_all = hidden.reshape(N_DP, TOK_REP, HIDDEN_SIZE)
    grad_all = out_grad.reshape(N_DP, TOK_REP, D_WIN)
    mom_all = momentum.reshape(N_DP, D_WIN, HIDDEN_SIZE)

    def replica(running, inputs):
        hid_rep, grad_rep, mom_rep = inputs
        gradient = lax.dot_general(grad_rep, hid_rep, (((0,), (0,)), ((), ())), preferred_element_type=jnp.float32)
        moment = DECAY * mom_rep.astype(jnp.float32) + gradient
        band_coef = forward_band(moment, band_tab)
        fresh_mom = (moment - inverse_band(band_coef, band_tab)).astype(jnp.bfloat16)
        return (running + band_coef, fresh_mom)
    start_sum = jnp.zeros((D_WIN // GROUP, BAND, HIDDEN_SIZE // GROUP, BAND), jnp.float32)
    summed, fresh_all = lax.scan(replica, start_sum, (hid_all, grad_all, mom_all))
    update = inverse_band(summed, band_tab).astype(jnp.bfloat16)
    return (fresh_all.reshape(N_DP * D_WIN, HIDDEN_SIZE), update)
```

```python
import jax
import jax.numpy as jnp
import ml_dtypes
import numpy as np
from jax import lax
from jax.experimental import pallas as pl
from jax.experimental.pallas import tpu as pltpu
from jax.sharding import PartitionSpec as P

MESH = pl.DeviceIdType.MESH
F32, BF16 = jnp.float32, jnp.bfloat16
GROUP, BAND, DECAY = 64, 16, 0.9
D_WIN, TOK, COLS = 2304, 1024, 1152
QTOK, HALF_TOK = 256, 512
NZ, NX, NDP = 8, 4, 64
SHARE = D_WIN // NDP
PADDED_SHARE = 40
BLOCKS = ((0, 512), (512, 512), (1024, 128))
BW = 384


def dct():
    k = np.arange(GROUP)[:, None].astype(np.float64)
    n = np.arange(GROUP)[None, :].astype(np.float64)
    scale = np.where(k == 0, np.sqrt(1.0 / GROUP), np.sqrt(2.0 / GROUP))
    return scale * np.cos(np.pi * (2.0 * n + 1.0) * k / (2.0 * GROUP))


def group_table(groups):
    c = dct()
    table = np.zeros((GROUP * groups, GROUP * groups))
    high = GROUP - BAND
    for g in range(groups):
        rows = slice(GROUP * g, GROUP * (g + 1))
        table[rows, BAND * g : BAND * (g + 1)] = c[:BAND].T
        first = BAND * groups + high * g
        table[rows, first : first + high] = c[BAND:].T
    return table


def halves(x):
    hi = x.astype(np.float32).astype(ml_dtypes.bfloat16)
    lo = (x - hi.astype(np.float64)).astype(np.float32).astype(ml_dtypes.bfloat16)
    return np.stack([hi, lo])


def share_table():
    c = dct()
    table = np.zeros((NDP, PADDED_SHARE, 2 * BAND), np.float32)
    for d in range(NDP):
        first = SHARE * d // GROUP
        for r in range(SHARE):
            pos = SHARE * d + r
            i = pos // GROUP - first
            table[d, r, BAND * i : BAND * (i + 1)] = c[:BAND, pos % GROUP]
    return table


def nn(a, b):
    return lax.dot_general(a, b, (((1,), (0,)), ((), ())), preferred_element_type=F32)


def tn(a, b):
    return lax.dot_general(a, b, (((0,), (0,)), ((), ())), preferred_element_type=F32)


def nt(a, b):
    return lax.dot_general(a, b, (((1,), (1,)), ((), ())), preferred_element_type=F32)


def split(x):
    hi = x.astype(BF16)
    return hi, (x - hi.astype(F32)).astype(BF16)


def three(op, a, b):
    return op(a[0], b[0]) + (op(a[1], b[0]) + op(a[0], b[1]))


def kernel(
    hid, og, mom, f8_in, f4_in, share_in,
    out, upd,
    f8, f4, share, og_all, h_all, mom_all, acc, wlo, whi, wh4, rlo, rhi, rh4,
    hp, band1, band, xr, xs, zr, zs, fin,
    l_sem, y_send, y_recv, f_send, f_recv, s_send, s_recv, x_send, x_recv, z_send, z_recv, fin_send, fin_recv,
):
    dp, mp = lax.axis_index("dp"), lax.axis_index("mp")
    z, h, x = dp // 8, (dp // 4) % 2, dp % 4
    l, c = mp // 2, mp % 2
    y_peer = (dp, (1 - l) * 2 + c)
    sib = (dp, l * 2 + 1 - c)
    x_peers = [(z * 8 + h * 4 + (x + o) % 4, mp) for o in range(1, 4)]
    z_peers = [(((z + o) % 8) * 8 + h * 4 + x, mp) for o in range(1, 8)]
    h_peer = (z * 8 + (1 - h) * 4 + x, mp)

    def rows(first, n, mult):
        return pl.ds(pl.multiple_of(first, mult), n)

    own = rows(mp * QTOK, QTOK, QTOK)
    yrows = rows(((1 - l) * 2 + c) * QTOK, QTOK, QTOK)
    loc = rows(l * HALF_TOK, HALF_TOK, HALF_TOK)
    rem = rows((1 - l) * HALF_TOK, HALF_TOK, HALF_TOK)

    def remote(src, dst, s, r, dev):
        return pltpu.make_async_remote_copy(
            src_ref=src, dst_ref=dst, send_sem=s, recv_sem=r, device_id=dev, device_id_type=MESH
        )

    loads = [
        pltpu.make_async_copy(og, og_all.at[own, :], l_sem.at[0]),
        pltpu.make_async_copy(f8_in, f8, l_sem.at[1]),
        pltpu.make_async_copy(f4_in, f4, l_sem.at[2]),
        pltpu.make_async_copy(hid, h_all, l_sem.at[3]),
        pltpu.make_async_copy(mom, mom_all, l_sem.at[4]),
        pltpu.make_async_copy(share_in.at[dp], share, l_sem.at[5]),
    ]
    for cp in loads:
        cp.start()
    fin[...] = jnp.zeros_like(fin)

    barrier = pltpu.get_barrier_semaphore()
    greeted = [y_peer, sib, h_peer] + x_peers + z_peers
    for dev in greeted:
        pl.semaphore_signal(barrier, inc=1, device_id=dev, device_id_type=MESH)
    loads[0].wait()
    loads[1].wait()
    loads[2].wait()
    for j in range(4):
        a = og_all[own, 512 * j : 512 * (j + 1)]
        wlo[j] = (nn(a, f8[0, :, 0:128]) + nn(a, f8[1, :, 0:128])).astype(BF16)
    a = og_all[own, 2048:2304]
    wlo[4] = (nn(a, f4[0, :, 0:128]) + nn(a, f4[1, :, 0:128])).astype(BF16)
    pl.semaphore_wait(barrier, len(greeted))

    sib_copy = remote(og, og_all.at[own, :], s_send, s_recv, sib)
    sib_copy.start()
    y_low = [remote(wlo.at[j], rlo.at[c, j], y_send.at[j], y_recv.at[j], y_peer) for j in range(5)]
    y_high = [remote(whi.at[k], rhi.at[k], y_send.at[5 + k], y_recv.at[5 + k], y_peer) for k in range(4)]
    y_high.append(remote(wh4, rh4, y_send.at[9], y_recv.at[9], y_peer))
    for cp in y_low:
        cp.start()
    for k in range(4):
        a = og_all[own, 512 * k : 512 * (k + 1)]
        whi[k] = (nn(a, f8[0, :, 128:512]) + nn(a, f8[1, :, 128:512])).astype(BF16)
        y_high[k].start()
    a = og_all[own, 2048:2304]
    wh4[...] = (nn(a, f4[0, :, 128:256]) + nn(a, f4[1, :, 128:256])).astype(BF16)
    y_high[4].start()

    loads[3].wait()
    loads[4].wait()
    sib_copy.wait_recv()

    def own_part(k, r0, n):
        for b, (c0, cn) in enumerate(BLOCKS):
            g = tn(og_all[loc, pl.ds(r0, n)], h_all[loc, c0 : c0 + cn])
            g = DECAY * mom_all[pl.ds(r0, n), c0 : c0 + cn].astype(F32) + g
            acc[pl.ds(r0, n), c0 : c0 + cn] = g
            left = three(tn, (f8[0, 0:n, 0:128], f8[1, 0:n, 0:128]), split(g))
            right = three(nn, split(left), (f8[0, 0:cn, 0:128], f8[1, 0:cn, 0:128]))
            band1[k, :, 128 * b : 128 * (b + 1)] = right

    def own_step(k, carry):
        own_part(k, pl.multiple_of(k * 512, 512), 512)
        return carry

    lax.fori_loop(0, 4, own_step, 0)
    own_part(4, 2048, 256)
    for b, (c0, cn) in enumerate(BLOCKS):
        a = h_all[rem, c0 : c0 + cn]
        p = nn(a, f8[0, 0:cn, 0:128]) + nn(a, f8[1, 0:cn, 0:128])
        hp[0, :, 128 * b : 128 * (b + 1)], hp[1, :, 128 * b : 128 * (b + 1)] = split(p)

    x_sends = []
    f_low = [remote(rlo.at[c, j], rlo.at[c, j], f_send.at[j], f_recv.at[j], sib) for j in range(5)]
    for j in range(5):
        y_low[j].wait_recv()
        f_low[j].start()
    for j in range(5):
        total = band1[j]
        f_low[j].wait_recv()
        for cc in range(2):
            w = rlo[cc, j]
            part = rows(cc * QTOK, QTOK, QTOK)
            total = total + (tn(w, hp[0, part, :]) + tn(w, hp[1, part, :]))
        band[j] = total
        n = 32 if j < 4 else 16
        for o in range(1, 4):
            theirs = rows(((x + o) % 4) * n, n, n)
            cp = remote(band.at[j, theirs, :], xr.at[j, o - 1, 0:n, :], x_send.at[j, o - 1], x_recv.at[j, o - 1], x_peers[o - 1])
            cp.start()
            x_sends.append(cp)

    def chunk(k, r0, n, high_ref, f):
        y_high[k].wait_recv()
        low, high = rlo[c, k], high_ref[...]
        ogy = nt(low, f[0, :, 0:128]) + nt(low, f[1, :, 0:128])
        ogy = ogy + (nt(high, f[0, :, 128:n]) + nt(high, f[1, :, 128:n]))
        og_all[yrows, r0 : r0 + n] = ogy.astype(BF16)
        there = og_all.at[yrows, r0 : r0 + n]
        fwd = remote(there, there, f_send.at[5 + k], f_recv.at[5 + k], sib)
        fwd.start()
        fwd.wait_recv()
        a = og_all[rem, r0 : r0 + n]
        ap = split(nn(a, f8[0, 0:n, 0:128]) + nn(a, f8[1, 0:n, 0:128]))
        for b, (c0, cn) in enumerate(BLOCKS):
            lanes = slice(128 * b, 128 * (b + 1))
            bandf = band1[k, :, lanes] + three(tn, ap, (hp[0, :, lanes], hp[1, :, lanes]))
            t1 = three(nt, split(bandf), (f8[0, 0:cn, 0:128], f8[1, 0:cn, 0:128]))
            restored = three(nn, (f8[0, 0:n, 0:128], f8[1, 0:n, 0:128]), split(t1))
            g = tn(a, h_all[rem, c0 : c0 + cn])
            out[r0 : r0 + n, c0 : c0 + cn] = (acc[r0 : r0 + n, c0 : c0 + cn] + g - restored).astype(BF16)
        return fwd

    forwards = list(f_low)
    forwards.append(chunk(0, 0, 512, rhi.at[0], f8))

    z_sends = []
    for j in range(5):
        n = 32 if j < 4 else 16
        for o in range(3):
            x_sends[3 * j + o].wait_recv()
        mine = rows(x * n, n, n)
        xs[j, 0:n, :] = band[j, mine, :] + xr[j, 0, 0:n, :] + xr[j, 1, 0:n, :] + xr[j, 2, 0:n, :]
        for q in range(n // 8):
            to = (4 * (j % 2) if j < 4 else 0) + q
            away = (to - z + 8) % 8
            cp = remote(
                xs.at[j, 8 * q : 8 * (q + 1), :],
                zr.at[j // 2, jnp.maximum(away - 1, 0)],
                z_send.at[j, q],
                z_recv.at[j // 2, jnp.maximum(away - 1, 0)],
                (to * 8 + h * 4 + x, mp),
            )
            z_sends.append((cp, away))

            @pl.when(away != 0)
            def _():
                cp.start()

    forwards.append(chunk(1, 512, 512, rhi.at[1], f8))
    forwards.append(chunk(2, 1024, 512, rhi.at[2], f8))

    fin_sends = []
    for t in range(3):
        j = z // 4 + 2 * t if t < 2 else 4
        q = z % 4 if t < 2 else z % 2
        group = 8 * j + 2 * x + q // 2 if t < 2 else 32 + x
        half = q % 2
        first, last = (64 * group) // 36, (64 * group + 63) // 36
        there = z < 2 if t == 2 else z >= 0

        @pl.when(there)
        def _():
            total = xs[j, rows(8 * q, 8, 8), :]
            for o in range(7):
                slot = zr.at[t, o]
                remote(slot, slot, z_send.at[0, 0], z_recv.at[t, o], z_peers[0]).wait_recv()
                total = total + zr[t, o]
            zs[t] = total

        for u in range(3):
            owner = jnp.minimum(first + u, NDP - 1)
            slot = (group - (36 * owner) // 64) * 2 + half
            slot = jnp.clip(slot, 0, 3)
            goes = there & (first + u <= last)
            cp = remote(zs.at[t], fin.at[h, slot], fin_send.at[t, u], fin_recv.at[h, slot], (owner, mp))
            at_home = pltpu.make_async_copy(zs.at[t], fin.at[h, slot], fin_recv.at[h, slot])
            fin_sends.append((cp, goes & (owner != dp)))

            @pl.when(goes & (owner != dp))
            def _():
                cp.start()

            @pl.when(goes & (owner == dp))
            def _():
                at_home.start()

    forwards.append(chunk(3, 1536, 512, rhi.at[3], f8))

    two = (36 * dp + 35) // 64 - (36 * dp) // 64
    for hh in range(2):
        for s in range(4):

            def arrived(hh=hh, s=s):
                slot = fin.at[hh, s]
                pltpu.make_async_copy(slot, slot, fin_recv.at[hh, s]).wait()

            if s < 2:
                arrived()
            else:
                pl.when(two == 1)(arrived)
    loads[5].wait()
    low = [fin[0, s] + fin[1, s] for s in range(4)]
    low = jnp.concatenate(low, axis=0)
    lefted = lax.dot_general(
        share[...], low, (((1,), (0,)), ((), ())), precision=lax.Precision.HIGHEST, preferred_element_type=F32
    )
    for b, (c0, cn) in enumerate(BLOCKS):
        u = three(nt, split(lefted[:, 128 * b : 128 * (b + 1)]), (f8[0, 0:cn, 0:128], f8[1, 0:cn, 0:128]))
        upd[:, c0 : c0 + cn] = u[0:SHARE].astype(BF16)

    forwards.append(chunk(4, 2048, 256, rh4, f4))

    sib_copy.wait_send()
    for cp in y_low + y_high + forwards + x_sends:
        cp.wait_send()
    for cp, away in z_sends:
        pl.when(away != 0)(cp.wait_send)
    for cp, goes in fin_sends:
        pl.when(goes)(cp.wait_send)


def body(hidden, out_grad, momentum):
    f8, f4 = halves(group_table(8)), halves(group_table(4))
    hbm = pl.BlockSpec(memory_space=pltpu.HBM)
    vmem = pl.BlockSpec(memory_space=pltpu.VMEM)
    dma = pltpu.SemaphoreType.DMA
    return pl.pallas_call(
        kernel,
        out_shape=(pltpu.VMEM((D_WIN, COLS), BF16), pltpu.VMEM((SHARE, COLS), BF16)),
        in_specs=[hbm] * 6,
        out_specs=(vmem, vmem),
        scratch_shapes=[
            pltpu.VMEM((2, 512, 512), BF16),
            pltpu.VMEM((2, 256, 256), BF16),
            pltpu.VMEM((PADDED_SHARE, 2 * BAND), F32),
            pltpu.VMEM((TOK, D_WIN), BF16),
            pltpu.VMEM((TOK, COLS), BF16),
            pltpu.VMEM((D_WIN, COLS), BF16),
            pltpu.VMEM((D_WIN, COLS), F32),
            pltpu.VMEM((5, QTOK, 128), BF16),
            pltpu.VMEM((4, QTOK, 384), BF16),
            pltpu.VMEM((QTOK, 128), BF16),
            pltpu.VMEM((2, 5, QTOK, 128), BF16),
            pltpu.VMEM((4, QTOK, 384), BF16),
            pltpu.VMEM((QTOK, 128), BF16),
            pltpu.VMEM((2, HALF_TOK, BW), BF16),
            pltpu.VMEM((5, 128, BW), F32),
            pltpu.VMEM((5, 128, BW), F32),
            pltpu.VMEM((5, 3, 32, BW), F32),
            pltpu.VMEM((5, 32, BW), F32),
            pltpu.VMEM((3, 7, 8, BW), F32),
            pltpu.VMEM((3, 8, BW), F32),
            pltpu.VMEM((2, 4, 8, BW), F32),
            dma((6,)), dma((10,)), dma((10,)), dma((10,)), dma((10,)), dma, dma,
            dma((5, 3)), dma((5, 3)), dma((5, 4)), dma((3, 7)), dma((3, 3)), dma((2, 4)),
        ],
        compiler_params=pltpu.CompilerParams(
            collective_id=0, has_side_effects=True, vmem_limit_bytes=54 * 2**20
        ),
        cost_estimate=pl.CostEstimate(flops=4 * 2 * TOK * D_WIN * COLS, bytes_accessed=16 * 2**20, transcendentals=0),
    )(hidden, out_grad, momentum, f8, f4, share_table())


def solution(mesh):
    return jax.shard_map(
        body,
        mesh=mesh,
        in_specs=(P("dp", "mp"), P(("dp", "mp"), None), P("dp", "mp")),
        out_specs=(P("dp", "mp"), P("dp", "mp")),
        check_vma=False,
    )
```

```python
import jax
import jax.numpy as jnp
import ml_dtypes
import numpy as np
from jax import lax
from jax.experimental import pallas as pl
from jax.experimental.pallas import tpu as pltpu
from jax.sharding import PartitionSpec as P

MESH = pl.DeviceIdType.MESH
F32, BF16 = jnp.float32, jnp.bfloat16
GROUP, BAND, DECAY = 64, 16, 0.9
D_WIN, TOK, COLS = 2304, 1024, 1152
QTOK, HALF_TOK = 256, 512
NZ, NX, NDP = 8, 4, 64
SHARE = D_WIN // NDP
PADDED_SHARE = 40
BLOCKS = ((0, 512), (512, 512), (1024, 128))
BW = 384


def dct():
    k = np.arange(GROUP)[:, None].astype(np.float64)
    n = np.arange(GROUP)[None, :].astype(np.float64)
    scale = np.where(k == 0, np.sqrt(1.0 / GROUP), np.sqrt(2.0 / GROUP))
    return scale * np.cos(np.pi * (2.0 * n + 1.0) * k / (2.0 * GROUP))


def group_table(groups):
    c = dct()
    table = np.zeros((GROUP * groups, GROUP * groups))
    high = GROUP - BAND
    for g in range(groups):
        rows = slice(GROUP * g, GROUP * (g + 1))
        table[rows, BAND * g : BAND * (g + 1)] = c[:BAND].T
        first = BAND * groups + high * g
        table[rows, first : first + high] = c[BAND:].T
    return table


def halves(x):
    hi = x.astype(np.float32).astype(ml_dtypes.bfloat16)
    lo = (x - hi.astype(np.float64)).astype(np.float32).astype(ml_dtypes.bfloat16)
    return np.stack([hi, lo])


def share_table():
    c = dct()
    table = np.zeros((NDP, PADDED_SHARE, 2 * BAND), np.float32)
    for d in range(NDP):
        first = SHARE * d // GROUP
        for r in range(SHARE):
            pos = SHARE * d + r
            i = pos // GROUP - first
            table[d, r, BAND * i : BAND * (i + 1)] = c[:BAND, pos % GROUP]
    return table


def nn(a, b):
    return lax.dot_general(a, b, (((1,), (0,)), ((), ())), preferred_element_type=F32)


def tn(a, b):
    return lax.dot_general(a, b, (((0,), (0,)), ((), ())), preferred_element_type=F32)


def nt(a, b):
    return lax.dot_general(a, b, (((1,), (1,)), ((), ())), preferred_element_type=F32)


def split(x):
    hi = x.astype(BF16)
    return hi, (x - hi.astype(F32)).astype(BF16)


def cat(parts, axis):
    return jnp.concatenate(parts, axis=axis)


def fold(x, n):
    return x[:, 0:n] + x[:, n : 2 * n]


def stacked(x, axis):
    hi, lo = split(x)
    return cat((hi, lo, hi), axis)


def tables():
    f8, f4 = group_table(8), group_table(4)
    low8, low4 = halves(f8[:, 0:128]), halves(f4[:, 0:64])
    wide = lambda m: np.concatenate(list(halves(m)), axis=1)
    fl = np.concatenate(list(low8), axis=1)
    kts = np.concatenate([low8[0].T, low8[0].T, low8[1].T], axis=0)
    fts = -np.concatenate([low4[0].T, low4[1].T, low4[0].T], axis=0)
    return (
        fl, wide(f8[:, 128:512]), wide(f4[:, 0:128]), wide(f4[:, 128:256]),
        wide(f8.T), wide(f4.T), kts, fts, share_table(),
    )


def kernel(
    hid, og, mom, fl_in, fh_in, f4a_in, f4b_in, i8_in, i4_in, kts_in, fts_in, share_in,
    out, upd,
    fl, fh, f4a, f4b, i8, i4, kts, share, ogx, hx, ext, mom_all, wlo, whi, wh4, rlo, rhi, rh4,
    hp, band1, band, xr, xs, zr, zs, fin,
    l_sem, y_send, y_recv, f_send, f_recv, s_send, s_recv, x_send, x_recv, z_send, z_recv, fin_send, fin_recv, go, know,
):
    dp, mp = lax.axis_index("dp"), lax.axis_index("mp")
    z, h, x = dp // 8, (dp // 4) % 2, dp % 4
    l, c = mp // 2, mp % 2
    y_peer = (dp, (1 - l) * 2 + c)
    sib = (dp, l * 2 + 1 - c)
    diag = (dp, (1 - l) * 2 + 1 - c)
    x_peers = [(z * 8 + h * 4 + (x + o) % 4, mp) for o in range(1, 4)]
    z_peers = [(((z + o) % 8) * 8 + h * 4 + x, mp) for o in range(1, 8)]
    h_peer = (z * 8 + (1 - h) * 4 + x, mp)

    def rows(first, n, mult):
        return pl.ds(pl.multiple_of(first, mult), n)

    own = rows(mp * QTOK, QTOK, QTOK)
    yrows = rows(((1 - l) * 2 + c) * QTOK, QTOK, QTOK)
    loc = rows(l * HALF_TOK, HALF_TOK, HALF_TOK)
    rem = rows((1 - l) * HALF_TOK, HALF_TOK, HALF_TOK)
    mine_c = rows(c * QTOK, QTOK, QTOK)

    def remote(src, dst, s, r, dev):
        return pltpu.make_async_remote_copy(
            src_ref=src, dst_ref=dst, send_sem=s, recv_sem=r, device_id=dev, device_id_type=MESH
        )

    def signal(sem, dev):
        pl.semaphore_signal(sem, inc=1, device_id=dev, device_id_type=MESH)

    fin[...] = jnp.zeros_like(fin)

    barrier = pltpu.get_barrier_semaphore()
    for first_core in (0, 2):

        @pl.when(mp != first_core)
        def _():
            signal(barrier, (dp, first_core))

    pairs = [(og, ogx.at[own, :]), (fl_in, fl), (f4a_in, f4a), (fh_in, fh), (f4b_in, f4b), (hid, hx.at[0:TOK, :])]
    pairs += [(mom.at[512 * k : min(512 * (k + 1), D_WIN), :], mom_all.at[512 * k : min(512 * (k + 1), D_WIN), :]) for k in range(5)]
    pairs += [(i8_in, i8), (i4_in, i4), (kts_in, kts), (share_in.at[dp], share)]
    pairs += [(fts_in, ogx.at[TOK : TOK + 192, 256 * k : 256 * (k + 1)]) for k in range(9)]
    loads = [pltpu.make_async_copy(a, b, l_sem.at[i]) for i, (a, b) in enumerate(pairs)]
    for cp in loads[:3]:
        cp.start()

    @pl.when(c == 0)
    def _():
        pl.semaphore_wait(barrier, 3)
        signal(go, sib)

    sib_copy = remote(og, ogx.at[own, :], s_send, s_recv, sib)
    y_low = [remote(wlo.at[j], rlo.at[j, mine_c, :], y_send.at[j], y_recv.at[j], y_peer) for j in range(5)]
    y_high = [remote(whi.at[k], rhi.at[k], y_send.at[5 + k], y_recv.at[5 + k], y_peer) for k in range(4)]
    y_high.append(remote(wh4, rh4, y_send.at[9], y_recv.at[9], y_peer))

    loads[0].wait()
    loads[1].wait()
    for j in range(4):
        wlo[j] = fold(nn(ogx[own, 512 * j : 512 * (j + 1)], fl[...]), 128).astype(BF16)
    loads[2].wait()
    wlo[4] = fold(nn(ogx[own, 2048:2304], f4a[...]), 128).astype(BF16)
    for cp in loads[3:]:
        cp.start()

    @pl.when(c == 1)
    def _():
        pl.semaphore_wait(go, 1)

    @pl.when(mp == 1)
    def _():
        for dev in z_peers:
            signal(barrier, dev)

    @pl.when(mp == 3)
    def _():
        for dev in x_peers + [h_peer]:
            signal(barrier, dev)

    for cp in y_low:
        cp.start()
    sib_copy.start()
    loads[3].wait()
    for k in range(4):
        whi[k] = fold(nn(ogx[own, 512 * k : 512 * (k + 1)], fh[...]), 384).astype(BF16)
        y_high[k].start()
    loads[4].wait()
    wh4[...] = fold(nn(ogx[own, 2048:2304], f4b[...]), 128).astype(BF16)
    y_high[4].start()

    loads[5].wait()
    for t in range(0, TOK, 512):
        for b, (c0, cn) in enumerate(BLOCKS):
            lanes = slice(128 * b, 128 * (b + 1))
            hp[0, t : t + 512, lanes], hp[1, t : t + 512, lanes] = split(fold(nn(hx[t : t + 512, c0 : c0 + cn], fl[0:cn, :]), 128))

    def token_band(r0, n, tokens):
        a = stacked(fold(nn(ogx[tokens, pl.ds(r0, n)], fl[0:n, :]), 128), 0)
        hi = hp[0, tokens, :]
        return tn(a, cat((hi, hi, hp[1, tokens, :]), 0))

    def own_band(k, r0, n):
        for b, (c0, cn) in enumerate(BLOCKS):
            xh, xl = split(DECAY * fold(nn(mom_all[pl.ds(r0, n), c0 : c0 + cn], fl[0:cn, :]), 128))
            both = tn(fl[0:n, :], xh)
            band1[k, :, 128 * b : 128 * (b + 1)] = both[0:128] + both[128:256] + tn(fl[0:n, 0:128], xl)
        band1[k] += token_band(r0, n, loc)

    @pl.when(mp == 1)
    def _():
        pl.semaphore_wait(barrier, 7)

    @pl.when(mp == 3)
    def _():
        pl.semaphore_wait(barrier, 4)

    @pl.when(c == 1)
    def _():
        for dev in (sib, y_peer, diag):
            signal(know, dev)
        pl.semaphore_wait(know, 1)

    @pl.when(c == 0)
    def _():
        pl.semaphore_wait(know, 2)

    x_sends = []
    f_low = [remote(rlo.at[j, mine_c, :], rlo.at[j, mine_c, :], f_send.at[j], f_recv.at[j], sib) for j in range(5)]
    def x_done(j):
        n = 32 if j < 4 else 16
        for o in range(3):
            x_sends[3 * j + o].wait_recv()
        mine = rows(x * n, n, n)
        xs[j, 0:n, :] = band[j, mine, :] + xr[j, 0, 0:n, :] + xr[j, 1, 0:n, :] + xr[j, 2, 0:n, :]
        for q in range(n // 8):
            to = (4 * (j % 2) if j < 4 else 0) + q
            away = (to - z + 8) % 8
            cp = remote(
                xs.at[j, 8 * q : 8 * (q + 1), :],
                zr.at[j // 2, jnp.maximum(away - 1, 0)],
                z_send.at[j, q],
                z_recv.at[j // 2, jnp.maximum(away - 1, 0)],
                (to * 8 + h * 4 + x, mp),
            )
            z_sends.append((cp, away))
            pl.when(away != 0)(cp.start)

    z_sends = []
    sib_copy.wait_recv()
    for j in range(5):
        y_low[j].wait_recv()
        f_low[j].start()
        loads[6 + j].wait()
        own_band(j, 512 * j, 512 if j < 4 else 256)
        f_low[j].wait_recv()
        w = rlo[j]
        band[j] = band1[j] + tn(cat((w, w), 0), cat((hp[0, rem, :], hp[1, rem, :]), 0))
        n = 32 if j < 4 else 16
        for o in range(1, 4):
            theirs = rows(((x + o) % 4) * n, n, n)
            cp = remote(band.at[j, theirs, :], xr.at[j, o - 1, 0:n, :], x_send.at[j, o - 1], x_recv.at[j, o - 1], x_peers[o - 1])
            cp.start()
            x_sends.append(cp)
        if j >= 3:
            x_done(j - 3)

    def chunk(k, r0, n, high_ref, table, *beside):
        y_high[k].wait_recv()
        w = cat((rlo[k, mine_c, :], high_ref[...]), 1)
        ogx[yrows, r0 : r0 + n] = fold(nn(w, table[...]), n).astype(BF16)
        there = ogx.at[yrows, r0 : r0 + n]
        fwd = remote(there, there, f_send.at[5 + k], f_recv.at[5 + k], sib)
        fwd.start()
        for step in beside:
            step()
        fwd.wait_recv()
        bandf = band1[k] + token_band(r0, n, rem)
        for b, (c0, cn) in enumerate(BLOCKS):
            t1 = nn(stacked(bandf[:, 128 * b : 128 * (b + 1)], 1), kts[:, 0:cn])
            hi, lo = split(t1)
            for u in range(n // 256):
                part = slice(64 * u, 64 * (u + 1))
                ext[u, :, c0 : c0 + cn] = cat((hi[part], hi[part], lo[part]), 0)
        for u in range(n // 256):
            r = slice(r0 + 256 * u, r0 + 256 * (u + 1))
            g = tn(ogx[:, r], cat((hx[...], ext[u]), 0))
            out[r, :] = (DECAY * mom_all[r, :].astype(F32) + g).astype(BF16)
        return fwd

    for cp in loads[11:]:
        cp.wait()
    forwards = list(f_low)
    fin_sends = []

    def z_done(t):
        j = z // 4 + 2 * t if t < 2 else 4
        q = z % 4 if t < 2 else z % 2
        group = 8 * j + 2 * x + q // 2 if t < 2 else 32 + x
        half = q % 2
        first, last = (64 * group) // 36, (64 * group + 63) // 36
        there = z < 2 if t == 2 else z >= 0

        @pl.when(there)
        def _():
            total = xs[j, rows(8 * q, 8, 8), :]
            for o in range(7):
                slot = zr.at[t, o]
                remote(slot, slot, z_send.at[0, 0], z_recv.at[t, o], z_peers[0]).wait_recv()
                total = total + zr[t, o]
            zs[t] = total

        for u in range(3):
            owner = jnp.minimum(first + u, NDP - 1)
            slot = (group - (36 * owner) // 64) * 2 + half
            slot = jnp.clip(slot, 0, 3)
            goes = there & (first + u <= last)
            cp = remote(zs.at[t], fin.at[h, slot], fin_send.at[t, u], fin_recv.at[h, slot], (owner, mp))
            at_home = pltpu.make_async_copy(zs.at[t], fin.at[h, slot], fin_recv.at[h, slot])
            fin_sends.append((cp, goes & (owner != dp)))

            @pl.when(goes & (owner != dp))
            def _():
                cp.start()

            @pl.when(goes & (owner == dp))
            def _():
                at_home.start()

    def update():
        two = (36 * dp + 35) // 64 - (36 * dp) // 64
        for hh in range(2):
            for s in range(4):

                def arrived(hh=hh, s=s):
                    slot = fin.at[hh, s]
                    pltpu.make_async_copy(slot, slot, fin_recv.at[hh, s]).wait()

                if s < 2:
                    arrived()
                else:
                    pl.when(two == 1)(arrived)
        low = [fin[0, s] + fin[1, s] for s in range(4)]
        low = jnp.concatenate(low, axis=0)
        lefted = lax.dot_general(
            share[...], low, (((1,), (0,)), ((), ())), precision=lax.Precision.HIGHEST, preferred_element_type=F32
        )
        for b, (c0, cn) in enumerate(BLOCKS):
            u = nn(stacked(lefted[:, 128 * b : 128 * (b + 1)], 1), kts[:, 0:cn])
            upd[:, c0 : c0 + cn] = u[0:SHARE].astype(BF16)

    forwards.append(chunk(0, 0, 512, rhi.at[0], i8, lambda: x_done(2)))
    forwards.append(chunk(1, 512, 512, rhi.at[1], i8, lambda: x_done(3), lambda: x_done(4)))
    forwards.append(chunk(2, 1024, 512, rhi.at[2], i8, lambda: z_done(0), lambda: z_done(1)))
    forwards.append(chunk(3, 1536, 512, rhi.at[3], i8, lambda: z_done(2)))
    forwards.append(chunk(4, 2048, 256, rh4, i4, update))

    sib_copy.wait_send()
    for cp in y_low + y_high + forwards + x_sends:
        cp.wait_send()
    for cp, away in z_sends:
        pl.when(away != 0)(cp.wait_send)
    for cp, goes in fin_sends:
        pl.when(goes)(cp.wait_send)


def body(hidden, out_grad, momentum):
    consts = tables()
    hbm = pl.BlockSpec(memory_space=pltpu.HBM)
    vmem = pl.BlockSpec(memory_space=pltpu.VMEM)
    dma = pltpu.SemaphoreType.DMA
    return pl.pallas_call(
        kernel,
        out_shape=(pltpu.VMEM((D_WIN, COLS), BF16), pltpu.VMEM((SHARE, COLS), BF16)),
        in_specs=[hbm] * (3 + len(consts)),
        out_specs=(vmem, vmem),
        scratch_shapes=[
            *[pltpu.VMEM(t.shape, BF16) for t in consts[:7]],
            pltpu.VMEM((PADDED_SHARE, 2 * BAND), F32),
            pltpu.VMEM((TOK + 192, D_WIN), BF16),
            pltpu.VMEM((TOK, COLS), BF16),
            pltpu.VMEM((2, 192, COLS), BF16),
            pltpu.VMEM((D_WIN, COLS), BF16),
            pltpu.VMEM((5, QTOK, 128), BF16),
            pltpu.VMEM((4, QTOK, 384), BF16),
            pltpu.VMEM((QTOK, 128), BF16),
            pltpu.VMEM((5, HALF_TOK, 128), BF16),
            pltpu.VMEM((4, QTOK, 384), BF16),
            pltpu.VMEM((QTOK, 128), BF16),
            pltpu.VMEM((2, TOK, BW), BF16),
            pltpu.VMEM((5, 128, BW), F32),
            pltpu.VMEM((5, 128, BW), F32),
            pltpu.VMEM((5, 3, 32, BW), F32),
            pltpu.VMEM((5, 32, BW), F32),
            pltpu.VMEM((3, 7, 8, BW), F32),
            pltpu.VMEM((3, 8, BW), F32),
            pltpu.VMEM((2, 4, 8, BW), F32),
            dma((24,)), dma((10,)), dma((10,)), dma((10,)), dma((10,)), dma, dma,
            dma((5, 3)), dma((5, 3)), dma((5, 4)), dma((3, 7)), dma((3, 3)), dma((2, 4)),
            pltpu.SemaphoreType.REGULAR, pltpu.SemaphoreType.REGULAR,
        ],
        compiler_params=pltpu.CompilerParams(
            collective_id=0, has_side_effects=True, vmem_limit_bytes=54 * 2**20
        ),
        cost_estimate=pl.CostEstimate(flops=4 * 2 * TOK * D_WIN * COLS, bytes_accessed=16 * 2**20, transcendentals=0),
    )(hidden, out_grad, momentum, *consts)


def solution(mesh):
    return jax.shard_map(
        body,
        mesh=mesh,
        in_specs=(P("dp", "mp"), P(("dp", "mp"), None), P("dp", "mp")),
        out_specs=(P("dp", "mp"), P("dp", "mp")),
        check_vma=False,
    )
```

```python
import jax
import jax.numpy as jnp
import ml_dtypes
import numpy as np
from jax import lax
from jax.experimental import pallas as pl
from jax.experimental.pallas import tpu as pltpu
from jax.sharding import PartitionSpec as P

MESH = pl.DeviceIdType.MESH
F32, BF16 = jnp.float32, jnp.bfloat16
GROUP, BAND, DECAY = 64, 16, 0.9
D_WIN, TOK, COLS = 2304, 1024, 1152
QTOK, HALF_TOK = 256, 512
NZ, NX, NDP = 8, 4, 64
SHARE = D_WIN // NDP
PADDED_SHARE = 40
BLOCKS = ((0, 512), (512, 512), (1024, 128))
BW = 384


def dct():
    k = np.arange(GROUP)[:, None].astype(np.float64)
    n = np.arange(GROUP)[None, :].astype(np.float64)
    scale = np.where(k == 0, np.sqrt(1.0 / GROUP), np.sqrt(2.0 / GROUP))
    return scale * np.cos(np.pi * (2.0 * n + 1.0) * k / (2.0 * GROUP))


def group_table(groups):
    c = dct()
    table = np.zeros((GROUP * groups, GROUP * groups))
    high = GROUP - BAND
    for g in range(groups):
        rows = slice(GROUP * g, GROUP * (g + 1))
        table[rows, BAND * g : BAND * (g + 1)] = c[:BAND].T
        first = BAND * groups + high * g
        table[rows, first : first + high] = c[BAND:].T
    return table


def halves(x):
    hi = x.astype(np.float32).astype(ml_dtypes.bfloat16)
    lo = (x - hi.astype(np.float64)).astype(np.float32).astype(ml_dtypes.bfloat16)
    return np.stack([hi, lo])


def share_table():
    c = dct()
    table = np.zeros((NDP, PADDED_SHARE, 2 * BAND), np.float32)
    for d in range(NDP):
        first = SHARE * d // GROUP
        for r in range(SHARE):
            pos = SHARE * d + r
            i = pos // GROUP - first
            table[d, r, BAND * i : BAND * (i + 1)] = c[:BAND, pos % GROUP]
    return table


def nn(a, b):
    return lax.dot_general(a, b, (((1,), (0,)), ((), ())), preferred_element_type=F32)


def tn(a, b):
    return lax.dot_general(a, b, (((0,), (0,)), ((), ())), preferred_element_type=F32)


def nt(a, b):
    return lax.dot_general(a, b, (((1,), (1,)), ((), ())), preferred_element_type=F32)


def split(x):
    hi = x.astype(BF16)
    return hi, (x - hi.astype(F32)).astype(BF16)


def cat(parts, axis):
    return jnp.concatenate(parts, axis=axis)


def fold(x, n):
    return x[:, 0:n] + x[:, n : 2 * n]


def stacked(x, axis):
    hi, lo = split(x)
    return cat((hi, lo, hi), axis)


def tables():
    f8, f4 = group_table(8), group_table(4)
    low8, low4 = halves(f8[:, 0:128]), halves(f4[:, 0:64])
    wide = lambda m: np.concatenate(list(halves(m)), axis=1)
    fl = np.concatenate(list(low8), axis=1)
    kts = np.concatenate([low8[0].T, low8[0].T, low8[1].T], axis=0)
    fts = -np.concatenate([low4[0].T, low4[1].T, low4[0].T], axis=0)
    return (
        fl, wide(f8[:, 128:512]), wide(f4[:, 0:128]), wide(f4[:, 128:256]),
        wide(f8.T), wide(f4.T), kts, fts, share_table(),
    )


def kernel(
    hid, og, mom, fl_in, fh_in, f4a_in, f4b_in, i8_in, i4_in, kts_in, fts_in, share_in,
    out, upd,
    fl, fh, f4a, f4b, i8, i4, kts, share, ogx, hx, ext, mom_all, acc, wlo, whi, wh4, rlo, rhi, rh4,
    hp, band1, band, xr, xs, zr, zs, fin,
    l_sem, y_send, y_recv, f_send, f_recv, s_send, s_recv, x_send, x_recv, z_send, z_recv, fin_send, fin_recv, go, know,
):
    dp, mp = lax.axis_index("dp"), lax.axis_index("mp")
    z, h, x = dp // 8, (dp // 4) % 2, dp % 4
    l, c = mp // 2, mp % 2
    y_peer = (dp, (1 - l) * 2 + c)
    sib = (dp, l * 2 + 1 - c)
    diag = (dp, (1 - l) * 2 + 1 - c)
    x_peers = [(z * 8 + h * 4 + (x + o) % 4, mp) for o in range(1, 4)]
    z_peers = [(((z + o) % 8) * 8 + h * 4 + x, mp) for o in range(1, 8)]
    h_peer = (z * 8 + (1 - h) * 4 + x, mp)

    def rows(first, n, mult):
        return pl.ds(pl.multiple_of(first, mult), n)

    own = rows(mp * QTOK, QTOK, QTOK)
    yrows = rows(((1 - l) * 2 + c) * QTOK, QTOK, QTOK)
    loc = rows(l * HALF_TOK, HALF_TOK, HALF_TOK)
    rem = rows((1 - l) * HALF_TOK, HALF_TOK, HALF_TOK)
    mine_c = rows(c * QTOK, QTOK, QTOK)

    def remote(src, dst, s, r, dev):
        return pltpu.make_async_remote_copy(
            src_ref=src, dst_ref=dst, send_sem=s, recv_sem=r, device_id=dev, device_id_type=MESH
        )

    def signal(sem, dev):
        pl.semaphore_signal(sem, inc=1, device_id=dev, device_id_type=MESH)

    fin[...] = jnp.zeros_like(fin)

    barrier = pltpu.get_barrier_semaphore()
    for first_core in (0, 2):

        @pl.when(mp != first_core)
        def _():
            signal(barrier, (dp, first_core))

    pairs = [(og.at[:, 0:512], ogx.at[own, 0:512]), (fl_in, fl), (f4a_in, f4a), (fh_in, fh), (f4b_in, f4b), (hid, hx.at[0:TOK, :])]
    pairs += [(mom.at[512 * k : min(512 * (k + 1), D_WIN), :], mom_all.at[512 * k : min(512 * (k + 1), D_WIN), :]) for k in range(5)]
    pairs += [(i8_in, i8), (i4_in, i4), (kts_in, kts), (share_in.at[dp], share)]
    pairs += [(fts_in, ogx.at[TOK : TOK + 192, 256 * k : 256 * (k + 1)]) for k in range(9)]
    pairs += [(og.at[:, 512:], ogx.at[own, 512:])]
    loads = [pltpu.make_async_copy(a, b, l_sem.at[i]) for i, (a, b) in enumerate(pairs)]
    for cp in loads[0:2] + loads[24:] + loads[2:4]:
        cp.start()

    @pl.when(c == 0)
    def _():
        pl.semaphore_wait(barrier, 3)
        signal(go, sib)

    sib_copy = remote(og, ogx.at[own, :], s_send, s_recv, sib)
    def y_low(j):
        return remote(wlo.at[j], rlo.at[j, mine_c, :], y_send.at[j], y_recv.at[j], y_peer)

    def y_high(k):
        a, b = (wh4, rh4) if isinstance(k, int) and k == 4 else (whi.at[k], rhi.at[k])
        return remote(a, b, y_send.at[5 + k], y_recv.at[5 + k], y_peer)

    def f_low(j):
        there = rlo.at[j, mine_c, :]
        return remote(there, there, f_send.at[j], f_recv.at[j], sib)

    def f_high(k, n):
        there = ogx.at[yrows, pl.ds(first_row(k), n)]
        return remote(there, there, f_send.at[5 + k], f_recv.at[5 + k], sib)

    def x_copy(j, o, n):
        theirs = rows(((x + o) % 4) * n, n, n)
        return remote(band.at[j, theirs, :], xr.at[j, o - 1, 0:n, :], x_send.at[j, o - 1], x_recv.at[j, o - 1], x_peers[o - 1])

    def first_row(k):
        return 512 * k if isinstance(k, int) else pl.multiple_of(512 * k, 512)

    def loop(first, last, step):
        def once(i, carry):
            step(i)
            return carry

        lax.fori_loop(first, last, once, 0)

    def low_rows(j):
        wlo[j] = fold(nn(ogx[own, pl.ds(first_row(j), 512)], fl[...]), 128).astype(BF16)
        y_low(j).start()

    @pl.when(c == 1)
    def _():
        pl.semaphore_wait(go, 1)

    loads[0].wait()
    loads[1].wait()
    loads[24].wait()
    loop(0, 4, low_rows)
    loads[2].wait()
    wlo[4] = fold(nn(ogx[own, 2048:2304], f4a[...]), 128).astype(BF16)
    y_low(4).start()
    sib_copy.start()
    for cp in loads[4:24]:
        cp.start()

    @pl.when(mp == 1)
    def _():
        for dev in z_peers:
            signal(barrier, dev)

    @pl.when(mp == 3)
    def _():
        for dev in x_peers + [h_peer]:
            signal(barrier, dev)

    loads[3].wait()
    def high_rows(k):
        whi[k] = fold(nn(ogx[own, pl.ds(first_row(k), 512)], fh[...]), 384).astype(BF16)
        y_high(k).start()

    loop(0, 4, high_rows)
    loads[4].wait()
    wh4[...] = fold(nn(ogx[own, 2048:2304], f4b[...]), 128).astype(BF16)
    y_high(4).start()

    loads[5].wait()
    def hidden_band(i):
        t = rows(512 * i, 512, 512)
        for b, (c0, cn) in enumerate(BLOCKS):
            lanes = slice(128 * b, 128 * (b + 1))
            hp[0, t, lanes], hp[1, t, lanes] = split(fold(nn(hx[t, c0 : c0 + cn], fl[0:cn, :]), 128))

    loop(0, 2, hidden_band)

    def token_band(r0, n, tokens):
        a = stacked(fold(nn(ogx[tokens, pl.ds(r0, n)], fl[0:n, :]), 128), 0)
        hi = hp[0, tokens, :]
        return tn(a, cat((hi, hi, hp[1, tokens, :]), 0))

    def own_band(k, r0, n):
        for b, (c0, cn) in enumerate(BLOCKS):
            xh, xl = split(DECAY * fold(nn(mom_all[pl.ds(r0, n), c0 : c0 + cn], fl[0:cn, :]), 128))
            both = tn(fl[0:n, :], xh)
            band1[k, :, 128 * b : 128 * (b + 1)] = both[0:128] + both[128:256] + tn(fl[0:n, 0:128], xl)
        band1[k] += token_band(r0, n, loc)

    def z_copy(j, q):
        to = (4 * (j % 2) if j < 4 else 0) + q
        away = (to - z + 8) % 8
        cp = remote(
            xs.at[j, 8 * q : 8 * (q + 1), :],
            zr.at[j // 2, jnp.maximum(away - 1, 0)],
            z_send.at[j, q],
            z_recv.at[j // 2, jnp.maximum(away - 1, 0)],
            (to * 8 + h * 4 + x, mp),
        )
        return cp, away

    def x_done(j):
        n = 32 if j < 4 else 16
        for o in range(3):
            x_copy(j, o + 1, n).wait_recv()
        mine = rows(x * n, n, n)
        xs[j, 0:n, :] = band[j, mine, :] + xr[j, 0, 0:n, :] + xr[j, 1, 0:n, :] + xr[j, 2, 0:n, :]
        for q in range(n // 8):
            cp, away = z_copy(j, q)
            pl.when(away != 0)(cp.start)

    sib_copy.wait_recv()
    for k in range(5):
        loads[6 + k].wait()

    def own_step(j, n=512):
        y_low(j).wait_recv()
        f_low(j).start()
        own_band(j, first_row(j), n)

    def send_step(j, n=512):
        f_low(j).wait_recv()
        w = rlo[j]
        band[j] = band1[j] + tn(cat((w, w), 0), cat((hp[0, rem, :], hp[1, rem, :]), 0))
        for o in range(1, 4):
            x_copy(j, o, n // 16).start()

    def both(j):
        own_step(j)
        send_step(j)

    loop(0, 2, own_step)

    @pl.when(mp == 1)
    def _():
        pl.semaphore_wait(barrier, 7)

    @pl.when(mp == 3)
    def _():
        pl.semaphore_wait(barrier, 4)

    @pl.when(c == 1)
    def _():
        for dev in (sib, y_peer, diag):
            signal(know, dev)
        pl.semaphore_wait(know, 1)

    @pl.when(c == 0)
    def _():
        pl.semaphore_wait(know, 2)

    loop(0, 2, send_step)
    loop(2, 4, both)
    own_step(4, 256)
    send_step(4, 256)

    def arrive(k, n, table):
        y_high(k).wait_recv()
        w = cat((rlo[k, mine_c, :], rhi[k] if n == 512 else rh4[...]), 1)
        ogx[yrows, pl.ds(first_row(k), n)] = fold(nn(w, table[...]), n).astype(BF16)
        f_high(k, n).start()

    def extend(k):
        for b, (c0, cn) in enumerate(BLOCKS):
            t1 = nn(stacked(band[k, :, 128 * b : 128 * (b + 1)], 1), kts[:, 0:cn])
            hi, lo = split(t1)
            for u in range(2):
                part = slice(64 * u, 64 * (u + 1))
                ext[u, :, c0 : c0 + cn] = cat((hi[part], hi[part], lo[part]), 0)

    def own_part(u, i):
        r = rows(256 * u, 256, 256)
        g = tn(cat((ogx[loc, r], ogx[TOK : TOK + 192, r]), 0), cat((hx[loc, :], ext[i]), 0))
        acc[r, :] = DECAY * mom_all[r, :].astype(F32) + g

    def fresh(u):
        r = rows(256 * u, 256, 256)
        out[r, :] = (acc[r, :] + tn(ogx[rem, r], hx[rem, :])).astype(BF16)

    for cp in loads[11:24]:
        cp.wait()
    def piece(t):
        j = z // 4 + 2 * t if t < 2 else 4
        q = z % 4 if t < 2 else z % 2
        group = 8 * j + 2 * x + q // 2 if t < 2 else 32 + x
        half = q % 2
        first, last = (64 * group) // 36, (64 * group + 63) // 36
        there = z < 2 if t == 2 else z >= 0
        return j, q, group, half, first, last, there

    def fin_copy(t, u):
        j, q, group, half, first, last, there = piece(t)
        owner = jnp.minimum(first + u, NDP - 1)
        slot = jnp.clip((group - (36 * owner) // 64) * 2 + half, 0, 3)
        goes = there & (first + u <= last)
        cp = remote(zs.at[t], fin.at[h, slot], fin_send.at[t, u], fin_recv.at[h, slot], (owner, mp))
        at_home = pltpu.make_async_copy(zs.at[t], fin.at[h, slot], fin_recv.at[h, slot])
        return cp, at_home, goes & (owner != dp), goes & (owner == dp)

    def z_done(t):
        j, q, group, half, first, last, there = piece(t)

        @pl.when(there)
        def _():
            total = xs[j, rows(8 * q, 8, 8), :]
            for o in range(7):
                slot = zr.at[t, o]
                remote(slot, slot, z_send.at[0, 0], z_recv.at[t, o], z_peers[0]).wait_recv()
                total = total + zr[t, o]
            zs[t] = total

        for u in range(3):
            cp, at_home, away, here = fin_copy(t, u)
            pl.when(away)(cp.start)
            pl.when(here)(at_home.start)

    def update():
        two = (36 * dp + 35) // 64 - (36 * dp) // 64
        for hh in range(2):
            for s in range(4):

                def arrived(hh=hh, s=s):
                    slot = fin.at[hh, s]
                    pltpu.make_async_copy(slot, slot, fin_recv.at[hh, s]).wait()

                if s < 2:
                    arrived()
                else:
                    pl.when(two == 1)(arrived)
        low = [fin[0, s] + fin[1, s] for s in range(4)]
        low = jnp.concatenate(low, axis=0)
        lefted = lax.dot_general(
            share[...], low, (((1,), (0,)), ((), ())), precision=lax.Precision.HIGHEST, preferred_element_type=F32
        )
        for b, (c0, cn) in enumerate(BLOCKS):
            u = nn(stacked(lefted[:, 128 * b : 128 * (b + 1)], 1), kts[:, 0:cn])
            upd[:, c0 : c0 + cn] = u[0:SHARE].astype(BF16)

    def chunk(k):
        arrive(k, 512, i8)
        extend(k)
        loop(0, 2, lambda i: own_part(2 * k + i, i))

        @pl.when(k == 0)
        def _():
            x_done(0)
            x_done(1)

        @pl.when(k == 1)
        def _():
            x_done(2)
            x_done(3)

        f_high(k, 512).wait_recv()
        fresh(2 * k)

        @pl.when(k == 3)
        def _():
            arrive(4, 256, i4)

        fresh(2 * k + 1)

        @pl.when(k == 1)
        def _():
            x_done(4)
            z_done(0)

        @pl.when(k == 2)
        def _():
            extend(4)
            own_part(8, 0)
            z_done(1)
            z_done(2)

    loop(0, 4, chunk)
    update()
    f_high(4, 256).wait_recv()
    fresh(8)

    sib_copy.wait_send()
    for k in range(5):
        y_low(k).wait_send()
        y_high(k).wait_send()
        f_low(k).wait_send()
        f_high(k, 512 if k < 4 else 256).wait_send()
        for o in range(1, 4):
            x_copy(k, o, 32 if k < 4 else 16).wait_send()
    for j in range(5):
        for q in range(4 if j < 4 else 2):
            cp, away = z_copy(j, q)
            pl.when(away != 0)(cp.wait_send)
    for t in range(3):
        for u in range(3):
            cp, at_home, away, here = fin_copy(t, u)
            pl.when(away)(cp.wait_send)


def body(hidden, out_grad, momentum):
    consts = tables()
    hbm = pl.BlockSpec(memory_space=pltpu.HBM)
    vmem = pl.BlockSpec(memory_space=pltpu.VMEM)
    dma = pltpu.SemaphoreType.DMA
    return pl.pallas_call(
        kernel,
        out_shape=(pltpu.VMEM((D_WIN, COLS), BF16), pltpu.VMEM((SHARE, COLS), BF16)),
        in_specs=[hbm] * (3 + len(consts)),
        out_specs=(vmem, vmem),
        scratch_shapes=[
            *[pltpu.VMEM(t.shape, BF16) for t in consts[:7]],
            pltpu.VMEM((PADDED_SHARE, 2 * BAND), F32),
            pltpu.VMEM((TOK + 192, D_WIN), BF16),
            pltpu.VMEM((TOK, COLS), BF16),
            pltpu.VMEM((2, 192, COLS), BF16),
            pltpu.VMEM((D_WIN, COLS), BF16),
            pltpu.VMEM((D_WIN, COLS), F32),
            pltpu.VMEM((5, QTOK, 128), BF16),
            pltpu.VMEM((4, QTOK, 384), BF16),
            pltpu.VMEM((QTOK, 128), BF16),
            pltpu.VMEM((5, HALF_TOK, 128), BF16),
            pltpu.VMEM((4, QTOK, 384), BF16),
            pltpu.VMEM((QTOK, 128), BF16),
            pltpu.VMEM((2, TOK, BW), BF16),
            pltpu.VMEM((5, 128, BW), F32),
            pltpu.VMEM((5, 128, BW), F32),
            pltpu.VMEM((5, 3, 32, BW), F32),
            pltpu.VMEM((5, 32, BW), F32),
            pltpu.VMEM((3, 7, 8, BW), F32),
            pltpu.VMEM((3, 8, BW), F32),
            pltpu.VMEM((2, 4, 8, BW), F32),
            dma((25,)), dma((10,)), dma((10,)), dma((10,)), dma((10,)), dma, dma,
            dma((5, 3)), dma((5, 3)), dma((5, 4)), dma((3, 7)), dma((3, 3)), dma((2, 4)),
            pltpu.SemaphoreType.REGULAR, pltpu.SemaphoreType.REGULAR,
        ],
        compiler_params=pltpu.CompilerParams(
            collective_id=0, has_side_effects=True, vmem_limit_bytes=54 * 2**20
        ),
        cost_estimate=pl.CostEstimate(flops=4 * 2 * TOK * D_WIN * COLS, bytes_accessed=16 * 2**20, transcendentals=0),
    )(hidden, out_grad, momentum, *consts)


def solution(mesh):
    return jax.shard_map(
        body,
        mesh=mesh,
        in_specs=(P("dp", "mp"), P(("dp", "mp"), None), P("dp", "mp")),
        out_specs=(P("dp", "mp"), P("dp", "mp")),
        check_vma=False,
    )
```

```python
import jax
import jax.numpy as jnp
import ml_dtypes
import numpy as np
from jax import lax
from jax.experimental import pallas as pl
from jax.experimental.pallas import tpu as pltpu
from jax.sharding import PartitionSpec as P

MESH = pl.DeviceIdType.MESH
F32, BF16 = jnp.float32, jnp.bfloat16
GROUP, BAND, DECAY = 64, 16, 0.9
D_WIN, TOK, COLS = 2304, 1024, 1152
QTOK, HALF_TOK = 256, 512
NZ, NX, NDP = 8, 4, 64
SHARE = D_WIN // NDP
PADDED_SHARE = 40
BLOCKS = ((0, 512), (512, 512), (1024, 128))
BW = 384


def dct():
    k = np.arange(GROUP)[:, None].astype(np.float64)
    n = np.arange(GROUP)[None, :].astype(np.float64)
    scale = np.where(k == 0, np.sqrt(1.0 / GROUP), np.sqrt(2.0 / GROUP))
    return scale * np.cos(np.pi * (2.0 * n + 1.0) * k / (2.0 * GROUP))


def group_table(groups):
    c = dct()
    table = np.zeros((GROUP * groups, GROUP * groups))
    high = GROUP - BAND
    for g in range(groups):
        rows = slice(GROUP * g, GROUP * (g + 1))
        table[rows, BAND * g : BAND * (g + 1)] = c[:BAND].T
        first = BAND * groups + high * g
        table[rows, first : first + high] = c[BAND:].T
    return table


def halves(x):
    hi = x.astype(np.float32).astype(ml_dtypes.bfloat16)
    lo = (x - hi.astype(np.float64)).astype(np.float32).astype(ml_dtypes.bfloat16)
    return np.stack([hi, lo])


def share_table():
    c = dct()
    table = np.zeros((NDP, PADDED_SHARE, 2 * BAND), np.float32)
    for d in range(NDP):
        first = SHARE * d // GROUP
        for r in range(SHARE):
            pos = SHARE * d + r
            i = pos // GROUP - first
            table[d, r, BAND * i : BAND * (i + 1)] = c[:BAND, pos % GROUP]
    return table


def nn(a, b):
    return lax.dot_general(a, b, (((1,), (0,)), ((), ())), preferred_element_type=F32)


def tn(a, b):
    return lax.dot_general(a, b, (((0,), (0,)), ((), ())), preferred_element_type=F32)


def nt(a, b):
    return lax.dot_general(a, b, (((1,), (1,)), ((), ())), preferred_element_type=F32)


def split(x):
    hi = x.astype(BF16)
    return hi, (x - hi.astype(F32)).astype(BF16)


def cat(parts, axis):
    return jnp.concatenate(parts, axis=axis)


def fold(x, n):
    return x[:, 0:n] + x[:, n : 2 * n]


def stacked(x, axis):
    hi, lo = split(x)
    return cat((hi, lo, hi), axis)


def tables():
    f8, f4 = group_table(8), group_table(4)
    low8, low4 = halves(f8[:, 0:128]), halves(f4[:, 0:64])
    wide = lambda m: np.concatenate(list(halves(m)), axis=1)
    fl = np.concatenate(list(low8), axis=1)
    kts = np.concatenate([low8[0].T, low8[0].T, low8[1].T], axis=0)
    fts = -np.concatenate([low4[0].T, low4[1].T, low4[0].T], axis=0)
    return (
        fl, wide(f8[:, 128:512]), wide(f4[:, 0:128]), wide(f4[:, 128:256]),
        wide(f8.T), wide(f4.T), kts, fts, share_table(),
    )


def kernel(
    hid, og, mom, fl_in, fh_in, f4a_in, f4b_in, i8_in, i4_in, kts_in, fts_in, share_in,
    out, upd,
    fl, fh, f4a, f4b, i8, i4, kts, share, ogx, hx, ext, mom_all, acc, wlo, whi, wh4, rlo, rhi, rh4,
    hp, band1, band, xr, xs, zr, zs, fin,
    l_sem, y_send, y_recv, f_send, f_recv, s_send, s_recv, x_send, x_recv, z_send, z_recv, fin_send, fin_recv, go, know,
):
    dp, mp = lax.axis_index("dp"), lax.axis_index("mp")
    z, h, x = dp // 8, (dp // 4) % 2, dp % 4
    l, c = mp // 2, mp % 2
    y_peer = (dp, (1 - l) * 2 + c)
    sib = (dp, l * 2 + 1 - c)
    diag = (dp, (1 - l) * 2 + 1 - c)
    x_peers = [(z * 8 + h * 4 + (x + o) % 4, mp) for o in range(1, 4)]
    z_peers = [(((z + o) % 8) * 8 + h * 4 + x, mp) for o in range(1, 8)]
    h_peer = (z * 8 + (1 - h) * 4 + x, mp)

    def rows(first, n, mult):
        return pl.ds(pl.multiple_of(first, mult), n)

    own = rows(mp * QTOK, QTOK, QTOK)
    yrows = rows(((1 - l) * 2 + c) * QTOK, QTOK, QTOK)
    loc = rows(l * HALF_TOK, HALF_TOK, HALF_TOK)
    rem = rows((1 - l) * HALF_TOK, HALF_TOK, HALF_TOK)
    mine_c = rows(c * QTOK, QTOK, QTOK)

    def remote(src, dst, s, r, dev):
        return pltpu.make_async_remote_copy(
            src_ref=src, dst_ref=dst, send_sem=s, recv_sem=r, device_id=dev, device_id_type=MESH
        )

    def signal(sem, dev):
        pl.semaphore_signal(sem, inc=1, device_id=dev, device_id_type=MESH)

    fin[...] = jnp.zeros_like(fin)

    barrier = pltpu.get_barrier_semaphore()
    for first_core in (0, 2):

        @pl.when(mp != first_core)
        def _():
            signal(barrier, (dp, first_core))

    pairs = [(og.at[:, 0:512], ogx.at[own, 0:512]), (fl_in, fl), (f4a_in, f4a), (fh_in, fh), (f4b_in, f4b), (hid, hx.at[0:TOK, :])]
    pairs += [(mom.at[512 * k : min(512 * (k + 1), D_WIN), :], mom_all.at[512 * k : min(512 * (k + 1), D_WIN), :]) for k in range(5)]
    pairs += [(i8_in, i8), (i4_in, i4), (kts_in, kts), (share_in.at[dp], share)]
    pairs += [(fts_in, ogx.at[TOK : TOK + 192, 256 * k : 256 * (k + 1)]) for k in range(9)]
    pairs += [(og.at[:, 512:], ogx.at[own, 512:])]
    loads = [pltpu.make_async_copy(a, b, l_sem.at[i]) for i, (a, b) in enumerate(pairs)]
    for cp in loads[0:2] + loads[24:] + loads[2:4]:
        cp.start()

    @pl.when(c == 0)
    def _():
        pl.semaphore_wait(barrier, 3)
        signal(go, sib)

    sib_copy = remote(og, ogx.at[own, :], s_send, s_recv, sib)
    def y_low(j):
        return remote(wlo.at[j], rlo.at[j, mine_c, :], y_send.at[j], y_recv.at[j], y_peer)

    def y_high(k):
        a, b = (wh4, rh4) if isinstance(k, int) and k == 4 else (whi.at[k], rhi.at[k])
        return remote(a, b, y_send.at[5 + k], y_recv.at[5 + k], y_peer)

    def f_low(j):
        there = rlo.at[j, mine_c, :]
        return remote(there, there, f_send.at[j], f_recv.at[j], sib)

    def f_high(k, n):
        there = ogx.at[yrows, pl.ds(first_row(k), n)]
        return remote(there, there, f_send.at[5 + k], f_recv.at[5 + k], sib)

    def x_copy(j, o, n):
        theirs = rows(((x + o) % 4) * n, n, n)
        return remote(band.at[j, theirs, :], xr.at[j, o - 1, 0:n, :], x_send.at[j, o - 1], x_recv.at[j, o - 1], x_peers[o - 1])

    def first_row(k):
        return 512 * k if isinstance(k, int) else pl.multiple_of(512 * k, 512)

    def loop(first, last, step):
        def once(i, carry):
            step(i)
            return carry

        lax.fori_loop(first, last, once, 0)

    def low_rows(j):
        wlo[j] = fold(nn(ogx[own, pl.ds(first_row(j), 512)], fl[...]), 128).astype(BF16)
        y_low(j).start()

    @pl.when(c == 1)
    def _():
        pl.semaphore_wait(go, 1)

    loads[0].wait()
    loads[1].wait()
    loads[24].wait()
    loop(0, 4, low_rows)
    loads[2].wait()
    wlo[4] = fold(nn(ogx[own, 2048:2304], f4a[...]), 128).astype(BF16)
    y_low(4).start()
    sib_copy.start()
    for cp in loads[4:24]:
        cp.start()

    @pl.when(mp == 1)
    def _():
        for dev in z_peers:
            signal(barrier, dev)

    @pl.when(mp == 3)
    def _():
        for dev in x_peers + [h_peer]:
            signal(barrier, dev)

    loads[3].wait()
    def high_rows(k):
        whi[k] = fold(nn(ogx[own, pl.ds(first_row(k), 512)], fh[...]), 384).astype(BF16)
        y_high(k).start()

    loop(0, 4, high_rows)
    loads[4].wait()
    wh4[...] = fold(nn(ogx[own, 2048:2304], f4b[...]), 128).astype(BF16)
    y_high(4).start()

    loads[5].wait()
    def hidden_band(i):
        t = rows(512 * i, 512, 512)
        for b, (c0, cn) in enumerate(BLOCKS):
            lanes = slice(128 * b, 128 * (b + 1))
            hp[0, t, lanes], hp[1, t, lanes] = split(fold(nn(hx[t, c0 : c0 + cn], fl[0:cn, :]), 128))

    loop(0, 2, hidden_band)

    def token_band(r0, n, tokens):
        a = stacked(fold(nn(ogx[tokens, pl.ds(r0, n)], fl[0:n, :]), 128), 0)
        hi = hp[0, tokens, :]
        return tn(a, cat((hi, hi, hp[1, tokens, :]), 0))

    def own_band(k, r0, n):
        for b, (c0, cn) in enumerate(BLOCKS):
            xh, xl = split(DECAY * fold(nn(mom_all[pl.ds(r0, n), c0 : c0 + cn], fl[0:cn, :]), 128))
            both = tn(fl[0:n, :], xh)
            band1[k, :, 128 * b : 128 * (b + 1)] = both[0:128] + both[128:256] + tn(fl[0:n, 0:128], xl)
        band1[k] += token_band(r0, n, loc)

    def z_copy(j, q):
        to = (4 * (j % 2) if j < 4 else 0) + q
        away = (to - z + 8) % 8
        cp = remote(
            xs.at[j, 8 * q : 8 * (q + 1), :],
            zr.at[j // 2, jnp.maximum(away - 1, 0)],
            z_send.at[j, q],
            z_recv.at[j // 2, jnp.maximum(away - 1, 0)],
            (to * 8 + h * 4 + x, mp),
        )
        return cp, away

    def x_done(j):
        n = 32 if j < 4 else 16
        for o in range(3):
            x_copy(j, o + 1, n).wait_recv()
        mine = rows(x * n, n, n)
        xs[j, 0:n, :] = band[j, mine, :] + xr[j, 0, 0:n, :] + xr[j, 1, 0:n, :] + xr[j, 2, 0:n, :]
        for q in range(n // 8):
            cp, away = z_copy(j, q)
            pl.when(away != 0)(cp.start)

    sib_copy.wait_recv()
    for k in range(5):
        loads[6 + k].wait()

    def own_step(j, n=512):
        y_low(j).wait_recv()
        f_low(j).start()
        own_band(j, first_row(j), n)

    def send_step(j, n=512):
        f_low(j).wait_recv()
        w = rlo[j]
        band[j] = band1[j] + tn(cat((w, w), 0), cat((hp[0, rem, :], hp[1, rem, :]), 0))
        for o in range(1, 4):
            x_copy(j, o, n // 16).start()

    def both(j):
        own_step(j)
        send_step(j)

    loop(0, 2, own_step)

    @pl.when(mp == 1)
    def _():
        pl.semaphore_wait(barrier, 7)

    @pl.when(mp == 3)
    def _():
        pl.semaphore_wait(barrier, 4)

    @pl.when(c == 1)
    def _():
        for dev in (sib, y_peer, diag):
            signal(know, dev)
        pl.semaphore_wait(know, 1)

    @pl.when(c == 0)
    def _():
        pl.semaphore_wait(know, 2)

    loop(0, 2, send_step)
    loop(2, 4, both)
    own_step(4, 256)
    send_step(4, 256)

    def arrive(k, n, table):
        y_high(k).wait_recv()
        w = cat((rlo[k, mine_c, :], rhi[k] if n == 512 else rh4[...]), 1)
        ogx[yrows, pl.ds(first_row(k), n)] = fold(nn(w, table[...]), n).astype(BF16)
        f_high(k, n).start()

    def extend(k):
        for b, (c0, cn) in enumerate(BLOCKS):
            t1 = nn(stacked(band[k, :, 128 * b : 128 * (b + 1)], 1), kts[:, 0:cn])
            hi, lo = split(t1)
            for u in range(2):
                part = slice(64 * u, 64 * (u + 1))
                ext[u, :, c0 : c0 + cn] = cat((hi[part], hi[part], lo[part]), 0)

    def own_part(u, i):
        r = rows(256 * u, 256, 256)
        g = tn(cat((ogx[loc, r], ogx[TOK : TOK + 192, r]), 0), cat((hx[loc, :], ext[i]), 0))
        acc[r, :] = DECAY * mom_all[r, :].astype(F32) + g

    def fresh(u):
        r = rows(256 * u, 256, 256)
        out[r, :] = (acc[r, :] + tn(ogx[rem, r], hx[rem, :])).astype(BF16)

    for cp in loads[11:24]:
        cp.wait()
    def piece(t):
        j = z // 4 + 2 * t if t < 2 else 4
        q = z % 4 if t < 2 else z % 2
        group = 8 * j + 2 * x + q // 2 if t < 2 else 32 + x
        half = q % 2
        first, last = (64 * group) // 36, (64 * group + 63) // 36
        there = z < 2 if t == 2 else z >= 0
        return j, q, group, half, first, last, there

    def fin_copy(t, u):
        j, q, group, half, first, last, there = piece(t)
        owner = jnp.minimum(first + u, NDP - 1)
        slot = jnp.clip((group - (36 * owner) // 64) * 2 + half, 0, 3)
        goes = there & (first + u <= last)
        cp = remote(zs.at[t], fin.at[h, slot], fin_send.at[t, u], fin_recv.at[h, slot], (owner, mp))
        at_home = pltpu.make_async_copy(zs.at[t], fin.at[h, slot], fin_recv.at[h, slot])
        return cp, at_home, goes & (owner != dp), goes & (owner == dp)

    def z_done(t):
        j, q, group, half, first, last, there = piece(t)

        @pl.when(there)
        def _():
            total = xs[j, rows(8 * q, 8, 8), :]
            for o in range(7):
                slot = zr.at[t, o]
                remote(slot, slot, z_send.at[0, 0], z_recv.at[t, o], z_peers[0]).wait_recv()
                total = total + zr[t, o]
            zs[t] = total

        for u in range(3):
            cp, at_home, away, here = fin_copy(t, u)
            pl.when(away)(cp.start)
            pl.when(here)(at_home.start)

    def update():
        two = (36 * dp + 35) // 64 - (36 * dp) // 64
        for hh in range(2):
            for s in range(4):

                def arrived(hh=hh, s=s):
                    slot = fin.at[hh, s]
                    pltpu.make_async_copy(slot, slot, fin_recv.at[hh, s]).wait()

                if s < 2:
                    arrived()
                else:
                    pl.when(two == 1)(arrived)
        low = [fin[0, s] + fin[1, s] for s in range(4)]
        low = jnp.concatenate(low, axis=0)
        lefted = lax.dot_general(
            share[...], low, (((1,), (0,)), ((), ())), precision=lax.Precision.HIGHEST, preferred_element_type=F32
        )
        for b, (c0, cn) in enumerate(BLOCKS):
            u = nn(stacked(lefted[:, 128 * b : 128 * (b + 1)], 1), kts[:, 0:cn])
            upd[:, c0 : c0 + cn] = u[0:SHARE].astype(BF16)

    def chunk(k):
        arrive(k, 512, i8)
        extend(k)
        loop(0, 2, lambda i: own_part(2 * k + i, i))

        @pl.when(k == 0)
        def _():
            x_done(0)
            x_done(1)

        @pl.when(k == 1)
        def _():
            x_done(2)
            x_done(3)
            x_done(4)

        @pl.when(k == 2)
        def _():
            z_done(0)
            z_done(1)
            extend(4)
            own_part(8, 0)

        f_high(k, 512).wait_recv()
        fresh(2 * k)

        @pl.when(k == 3)
        def _():
            arrive(4, 256, i4)

        fresh(2 * k + 1)

        @pl.when(k == 2)
        def _():
            z_done(2)

    loop(0, 4, chunk)
    update()
    f_high(4, 256).wait_recv()
    fresh(8)

    sib_copy.wait_send()
    for k in range(5):
        y_low(k).wait_send()
        y_high(k).wait_send()
        f_low(k).wait_send()
        f_high(k, 512 if k < 4 else 256).wait_send()
        for o in range(1, 4):
            x_copy(k, o, 32 if k < 4 else 16).wait_send()
    for j in range(5):
        for q in range(4 if j < 4 else 2):
            cp, away = z_copy(j, q)
            pl.when(away != 0)(cp.wait_send)
    for t in range(3):
        for u in range(3):
            cp, at_home, away, here = fin_copy(t, u)
            pl.when(away)(cp.wait_send)


def body(hidden, out_grad, momentum):
    consts = tables()
    hbm = pl.BlockSpec(memory_space=pltpu.HBM)
    vmem = pl.BlockSpec(memory_space=pltpu.VMEM)
    dma = pltpu.SemaphoreType.DMA
    return pl.pallas_call(
        kernel,
        out_shape=(pltpu.VMEM((D_WIN, COLS), BF16), pltpu.VMEM((SHARE, COLS), BF16)),
        in_specs=[hbm] * (3 + len(consts)),
        out_specs=(vmem, vmem),
        scratch_shapes=[
            *[pltpu.VMEM(t.shape, BF16) for t in consts[:7]],
            pltpu.VMEM((PADDED_SHARE, 2 * BAND), F32),
            pltpu.VMEM((TOK + 192, D_WIN), BF16),
            pltpu.VMEM((TOK, COLS), BF16),
            pltpu.VMEM((2, 192, COLS), BF16),
            pltpu.VMEM((D_WIN, COLS), BF16),
            pltpu.VMEM((D_WIN, COLS), F32),
            pltpu.VMEM((5, QTOK, 128), BF16),
            pltpu.VMEM((4, QTOK, 384), BF16),
            pltpu.VMEM((QTOK, 128), BF16),
            pltpu.VMEM((5, HALF_TOK, 128), BF16),
            pltpu.VMEM((4, QTOK, 384), BF16),
            pltpu.VMEM((QTOK, 128), BF16),
            pltpu.VMEM((2, TOK, BW), BF16),
            pltpu.VMEM((5, 128, BW), F32),
            pltpu.VMEM((5, 128, BW), F32),
            pltpu.VMEM((5, 3, 32, BW), F32),
            pltpu.VMEM((5, 32, BW), F32),
            pltpu.VMEM((3, 7, 8, BW), F32),
            pltpu.VMEM((3, 8, BW), F32),
            pltpu.VMEM((2, 4, 8, BW), F32),
            dma((25,)), dma((10,)), dma((10,)), dma((10,)), dma((10,)), dma, dma,
            dma((5, 3)), dma((5, 3)), dma((5, 4)), dma((3, 7)), dma((3, 3)), dma((2, 4)),
            pltpu.SemaphoreType.REGULAR, pltpu.SemaphoreType.REGULAR,
        ],
        compiler_params=pltpu.CompilerParams(
            collective_id=0, has_side_effects=True, vmem_limit_bytes=54 * 2**20
        ),
        cost_estimate=pl.CostEstimate(flops=4 * 2 * TOK * D_WIN * COLS, bytes_accessed=16 * 2**20, transcendentals=0),
    )(hidden, out_grad, momentum, *consts)


def solution(mesh):
    return jax.shard_map(
        body,
        mesh=mesh,
        in_specs=(P("dp", "mp"), P(("dp", "mp"), None), P("dp", "mp")),
        out_specs=(P("dp", "mp"), P("dp", "mp")),
        check_vma=False,
    )
```
